32 devices in a mesh: node: 2 (over core), trow: 4 (over y, x), tcol: 4 (over z).
Axes of the slice: x: 2, y: 2, z: 4, core: 2. Of those that a mesh axis runs over, the one named last changes fastest.
Arguments:
- near_blocks: bfloat16 [128, 8, 256, 256], P(('node', 'trow'), 'tcol'), may hold values from -27 to 75, as said below
- leaf_bases: bfloat16 [128, 256, 256], P(('node', 'trow')), may hold values from -1 to 1, as said below
- upper_bases: bfloat16 [64, 256, 256], P(('node', 'trow', 'tcol')), may hold values from -1 to 1, as said below
- neighbours: int32 [128, 8], P(('node', 'trow'), 'tcol'), may hold values from 0 to 127, as said below
Outputs:
- skeleton: float32 [128, 8, 128, 128], P(('node', 'trow'), 'tcol')
- upper_skeleton: float32 [64, 5, 128, 128], P(('node', 'trow', 'tcol'))
The draws below stay inside these ranges and needn't reach their ends.
Inputs may be any that keep to these rules, and one draw needn't show every extreme that they name: `neighbours`: slot 0 of row i is i, slot 1 is its sibling i XOR 1, and slots 2 to 7 are six distinct leaves among 2 (i // 2) - 4, -3, -2, -1, +2, +3, +4, +5, taken modulo 128. near_blocks[i, 0] is symmetric and positive definite. `leaf_bases`: each leaf basis is an orthogonal matrix rounded to bfloat16. `upper_bases`: each node basis is an orthogonal matrix rounded to bfloat16.
All inputs are finite; a program needn't handle non-finite values.
Results may differ from the reference program's by a relative error of at most 0.0038.
Values may be sent and summed in bfloat16 or wider, within the bound.
No kernel may reach another device: no remote copies, remote signals or barrier semaphores. Data moves between devices by JAX's collectives and lax.ppermute only.
A program may use at most 64 MiB of HBM per device.

```python
import math
import jax
import jax.numpy as jnp
from jax import lax

BLK = 256
RANK = 128
LEAVES = 128
PARENTS = 64


def draw_near_blocks(key, part):
    first_key = jax.random.fold_in(jax.random.fold_in(key, 11), 0)
    frame_key = jax.random.fold_in(key, 31)
    level_key = jax.random.fold_in(key, 37)
    shape = (LEAVES, 8, BLK, BLK)
    root = math.sqrt(BLK)
    noise = 0.5 * jnp.clip(jax.random.normal(first_key, shape, jnp.float32), -4.0, 4.0)
    levels = root * jax.random.uniform(level_key, (LEAVES, BLK), jnp.float32, 1.5, 4.5)
    frame_draw = jax.random.normal(frame_key, (LEAVES, BLK, BLK), jnp.float32)
    frame, upper = jnp.linalg.qr(frame_draw)
    graded = jnp.einsum('lab,lb,lcb->lac', frame, levels, frame, precision=lax.Precision.HIGHEST)
    graded = 0.5 * (graded + jnp.swapaxes(graded, 1, 2))
    diagonal = 0.5 * (noise[:, 0] + jnp.swapaxes(noise[:, 0], 1, 2)) + graded
    return noise.at[:, 0].set(diagonal).astype(jnp.bfloat16)


def orthogonal(key, count, order):
    normal_draw = jax.random.normal(key, (count, order, order), jnp.float32)
    basis, upper = jnp.linalg.qr(normal_draw)
    return basis.astype(jnp.bfloat16)


def draw_leaf_bases(key, part):
    return orthogonal(jax.random.fold_in(key, 17), LEAVES, BLK)


def draw_upper_bases(key, part):
    return orthogonal(jax.random.fold_in(key, 23), PARENTS, 2 * RANK)


def draw_neighbours(key, part):
    leaf_ids = jnp.arange(LEAVES, dtype=jnp.int32)
    base_key = jax.random.fold_in(key, 29)
    row_keys = jax.vmap(lambda leaf: jax.random.fold_in(base_key, leaf))(leaf_ids)
    orders = jax.vmap(lambda row_key: jax.random.permutation(row_key, 8))(row_keys)
    offsets = jnp.array([-4, -3, -2, -1, 2, 3, 4, 5], jnp.int32)
    starts = leaf_ids // 2 * 2
    picks = (starts[:, None] + offsets[orders[:, :6]]) % LEAVES
    return jnp.concatenate([leaf_ids[:, None], (leaf_ids ^ 1)[:, None], picks], axis=1).astype(jnp.int32)


def setup_inputs(seed: int = 0) -> dict:
    streams_of = jax.random.split(jax.random.key(seed), 5)
    near_blocks = draw_near_blocks(jax.random.fold_in(streams_of[4], 71), 0)
    leaf_bases = draw_leaf_bases(jax.random.fold_in(streams_of[4], 71), 0)
    upper_bases = draw_upper_bases(jax.random.fold_in(streams_of[4], 71), 0)
    neighbours = draw_neighbours(jax.random.fold_in(streams_of[4], 71), 0)
    return dict(near_blocks=near_blocks, leaf_bases=leaf_bases, upper_bases=upper_bases, neighbours=neighbours)


def eliminate(rotated, spare_size):
    corner = rotated[..., :spare_size, :spare_size]
    factor = jnp.linalg.cholesky(0.5 * (corner + jnp.swapaxes(corner, -1, -2)))
    coupled = lax.linalg.triangular_solve(factor, rotated[..., :spare_size, spare_size:], left_side=True, lower=True)
    return (factor, coupled)

def reduce_one(rotated, factor, coupled, spare_size):
    widened = jnp.broadcast_to(factor, (rotated.shape[0],) + factor.shape)
    solved = lax.linalg.triangular_solve(widened, rotated[:, :spare_size, spare_size:], left_side=True, lower=True)
    return rotated[:, spare_size:, spare_size:] - jnp.einsum('xr,kxs->krs', coupled, solved, precision=lax.Precision.HIGHEST)

def reference(near_blocks, leaf_bases, upper_bases, neighbours):
    spare_size = BLK - RANK

    def leaf_row(item):
        blocks_row, basis_row, leaf_list = item
        partner = leaf_bases[leaf_list].astype(jnp.float32)
        turned = jnp.einsum('kab,kbc->kac', blocks_row.astype(jnp.float32), partner, precision=lax.Precision.HIGHEST).astype(jnp.bfloat16)
        turned = lax.optimization_barrier(turned)
        rotated = jnp.einsum('ba,kbc->kac', basis_row.astype(jnp.float32), turned.astype(jnp.float32), precision=lax.Precision.HIGHEST)
        factor, coupled = eliminate(rotated[0], spare_size)
        return reduce_one(rotated, factor, coupled, spare_size)
    skeleton = lax.map(leaf_row, (near_blocks, leaf_bases, neighbours))
    packed = skeleton.astype(jnp.bfloat16)
    leaf_ids = jnp.arange(LEAVES, dtype=jnp.int32)
    target = 2 * ((neighbours // 2 - leaf_ids[:, None] // 2 + 2) % PARENTS) + neighbours % 2
    labels = jnp.arange(10, dtype=jnp.int32)
    parent_ids = jnp.arange(PARENTS, dtype=jnp.int32)

    def parent_row(item):
        parent, pair_blocks, pair_target, basis_row = item
        selector = (pair_target[:, :, None] == labels).astype(jnp.float32)
        blocks = jnp.einsum('akc,akxy->acxy', selector, pair_blocks.astype(jnp.float32), precision=lax.Precision.HIGHEST)
        merged = blocks.reshape(2, 5, 2, RANK, RANK).transpose(1, 0, 3, 2, 4).reshape(5, 2 * RANK, 2 * RANK).astype(jnp.bfloat16)
        merged = lax.optimization_barrier(merged)
        offsets = (parent + jnp.arange(5, dtype=jnp.int32) - 2) % PARENTS
        partners = upper_bases[offsets.astype(jnp.int32)].astype(jnp.float32)
        upper_mixed = jnp.einsum('dab,dbc->dac', merged.astype(jnp.float32), partners, precision=lax.Precision.HIGHEST).astype(jnp.bfloat16)
        upper_mixed = lax.optimization_barrier(upper_mixed)
        lifted = jnp.einsum('ba,dbc->dac', basis_row.astype(jnp.float32), upper_mixed.astype(jnp.float32), precision=lax.Precision.HIGHEST)
        factor, coupled = eliminate(lifted[2], RANK)
        return reduce_one(lifted, factor, coupled, RANK)
    upper_skeleton = lax.map(parent_row, (parent_ids, packed.reshape(PARENTS, 2, 8, RANK, RANK), target.reshape(PARENTS, 2, 8), upper_bases))
    return (skeleton, upper_skeleton)
```

```python
import functools

import jax
import jax.numpy as jnp
from jax import lax
from jax.experimental import pallas as pl
from jax.experimental.pallas import tpu as pltpu
from jax.sharding import PartitionSpec as P

BLK = 256
RANK = 128
SPARE = BLK - RANK
REACH = 4
PANEL = 32
F32 = jnp.float32
BF16 = jnp.bfloat16
VMEM = pltpu.VMEM
SMEM = pltpu.SMEM
PARAMS = pltpu.CompilerParams(vmem_limit_bytes=40 << 20)


def ring(array, axes, step):
    count = lax.axis_size(axes)
    return lax.ppermute(array, axes, [(i, (i + step) % count) for i in range(count)])


def split(x):
    high = x.astype(BF16)
    return high, (x - high.astype(F32)).astype(BF16)


def dot(a, b):
    return jnp.dot(a, b, preferred_element_type=F32)


def dot_t(a, b):
    return lax.dot_general(a, b, (((0,), (0,)), ((), ())), preferred_element_type=F32)


def dot3(a, b):
    a_high, a_low = split(a)
    b_high, b_low = split(b)
    return dot(
        jnp.concatenate([a_high, a_high, a_low], axis=1),
        jnp.concatenate([b_high, b_low, b_high], axis=0),
    )


def invert_small(x, order, count):
    ids = lax.broadcasted_iota(jnp.int32, (order, count), 0)
    x = list(x)
    for p in range(order):
        pivot = 1.0 / x[p][p : p + 1, :]
        here = ids == p
        row = jnp.where(here, 1.0, x[p])
        for i in range(order):
            if i != p:
                x[i] = jnp.where(here, 0.0, x[i]) - (x[i][p : p + 1, :] * pivot) * row
        x[p] = row * pivot
    return x


def solve_spd(left, right, inverse, count, size):
    for lo in range(0, size, PANEL):
        hi = lo + PANEL
        last = hi == size
        x = [
            jnp.transpose(left[pl.ds(lo + i, count, stride=size), :])[lo:hi, :]
            for i in range(PANEL)
        ]
        x = invert_small(x, PANEL, count)
        rest = jnp.zeros((size - PANEL, count), F32)
        for i in range(PANEL):
            inverse[pl.ds(i, count, stride=PANEL), :] = jnp.transpose(
                jnp.concatenate([x[i], rest], axis=0)
            )
        for item in range(count):
            base = item * size
            rows = slice(base + lo, base + hi)
            panel = right[rows, :]
            if not last:
                panel = jnp.concatenate([left[rows, :], panel], axis=1)
            panel = dot3(inverse[item * PANEL : (item + 1) * PANEL, :PANEL], panel)
            for start, stop in ((0, lo), (hi, size)):
                if start < stop:
                    part = slice(base + start, base + stop)
                    update = dot3(left[part, lo:hi], panel)
                    if not last:
                        left[part, :] -= update[:, :size]
                    right[part, :] -= update[:, -size:]
            if not last:
                left[rows, :] = panel[:, :size]
            right[rows, :] = panel[:, -size:]


def factor_kernel(count, group, tcol, block, basis, high, low, left, right, inverse):
    step = pl.program_id(0)

    @pl.when(tcol[0] == 0)
    def _():
        for g in range(group):
            turned = dot(block[g], basis[g]).astype(BF16)
            rotated = dot_t(basis[g][:, :SPARE], turned)
            corner = rotated[:, :SPARE]
            where = pl.ds(pl.multiple_of((step * group + g) * SPARE, SPARE), SPARE)
            left[where, :] = 0.5 * (corner + jnp.transpose(corner))
            right[where, :] = rotated[:, SPARE:]

        @pl.when(step == pl.num_programs(0) - 1)
        def _():
            solve_spd(left, right, inverse, count, SPARE)
            for item in range(count):
                solved = jnp.transpose(right[item * SPARE : (item + 1) * SPARE, :])
                high[item], low[item] = split(solved)

    @pl.when((tcol[0] != 0) & (step == 0))
    def _():
        high[...] = jnp.zeros_like(high)
        low[...] = jnp.zeros_like(low)


def factor(tcol, near_blocks, bases):
    count = bases.shape[0]
    group = 4
    whole = pl.BlockSpec((count, RANK, SPARE), lambda i: (0, 0, 0))
    shape = jax.ShapeDtypeStruct((count, RANK, SPARE), BF16)
    return pl.pallas_call(
        functools.partial(factor_kernel, count, group),
        grid=(count // group,),
        in_specs=[
            pl.BlockSpec(memory_space=SMEM),
            pl.BlockSpec((group, None, BLK, BLK), lambda i: (i, 0, 0, 0)),
            pl.BlockSpec((group, BLK, BLK), lambda i: (i, 0, 0)),
        ],
        out_specs=[whole, whole],
        out_shape=[shape, shape],
        scratch_shapes=[
            VMEM((count * SPARE, SPARE), F32),
            VMEM((count * SPARE, SPARE), F32),
            VMEM((count * PANEL, SPARE), F32),
        ],
        compiler_params=PARAMS,
        name="factor",
    )(tcol, near_blocks, bases)


def rotate_kernel(slots, group, position, block, basis, partners, upper, lower):
    step = pl.program_id(0)
    for g in range(group):
        turned = jnp.concatenate(
            [
                dot(block[g, k], partners[position[step * group + g, k]]).astype(BF16)
                for k in range(slots)
            ],
            axis=1,
        )
        rotated = dot_t(basis[g], turned)
        upper[g, :SPARE], upper[g, SPARE:] = split(rotated[:SPARE])
        lower[g] = rotated[SPARE:]


def rotate(position, near_blocks, bases, partners):
    count, slots = near_blocks.shape[:2]
    group = 2
    width = slots * RANK
    return pl.pallas_call(
        functools.partial(rotate_kernel, slots, group),
        grid=(count // group,),
        in_specs=[
            pl.BlockSpec(memory_space=SMEM),
            pl.BlockSpec((group, slots, BLK, BLK), lambda i: (i, 0, 0, 0)),
            pl.BlockSpec((group, BLK, BLK), lambda i: (i, 0, 0)),
            pl.BlockSpec(partners.shape, lambda i: (0, 0, 0)),
        ],
        out_specs=[
            pl.BlockSpec((group, 2 * SPARE, width), lambda i: (i, 0, 0)),
            pl.BlockSpec((group, RANK, width), lambda i: (i, 0, 0)),
        ],
        out_shape=[
            jax.ShapeDtypeStruct((count, 2 * SPARE, width), BF16),
            jax.ShapeDtypeStruct((count, RANK, width), F32),
        ],
        compiler_params=PARAMS,
        cost_estimate=pl.CostEstimate(
            flops=4 * count * slots * BLK * BLK * RANK * 2, bytes_accessed=12 << 20, transcendentals=0
        ),
        name="rotate",
    )(position, near_blocks, bases, partners)


def reduce_kernel(slots, group, high, low, upper, lower, skeleton, packed):
    for g in range(group):
        update = dot(jnp.concatenate([high[g], high[g]], axis=1), upper[g])
        update += dot(low[g], upper[g, :SPARE])
        result = lower[g] - update
        for k in range(slots):
            part = result[:, k * RANK : (k + 1) * RANK]
            skeleton[g, k] = part
            packed[g, k] = part.astype(BF16)


def reduce_rows(high, low, upper, lower):
    count, _, width = lower.shape
    slots = width // RANK
    group = 4
    solved = pl.BlockSpec((group, RANK, SPARE), lambda i: (i, 0, 0))
    blocks = pl.BlockSpec((group, slots, RANK, RANK), lambda i: (i, 0, 0, 0))
    shape = (count, slots, RANK, RANK)
    return pl.pallas_call(
        functools.partial(reduce_kernel, slots, group),
        grid=(count // group,),
        in_specs=[
            solved,
            solved,
            pl.BlockSpec((group, 2 * SPARE, width), lambda i: (i, 0, 0)),
            pl.BlockSpec((group, RANK, width), lambda i: (i, 0, 0)),
        ],
        out_specs=[blocks, blocks],
        out_shape=[jax.ShapeDtypeStruct(shape, F32), jax.ShapeDtypeStruct(shape, BF16)],
        compiler_params=PARAMS,
        name="reduce_rows",
    )(high, low, upper, lower)


def upper_kernel(parents, slots, target, blocks, basis, partners, out, merged, left, right, inverse):
    merged[...] = jnp.zeros_like(merged)
    for p in range(parents):
        for a in range(2):
            for k in range(slots):
                merged[p, target[2 * p + a, k], a * RANK : (a + 1) * RANK] = blocks[2 * p + a, k]
    lifted = []
    for p in range(parents):
        mixed = []
        for d in (2, 0, 1, 3, 4):
            pair = jnp.concatenate([merged[p, 2 * d], merged[p, 2 * d + 1]], axis=1)
            partner = basis[p] if d == 2 else partners[p + d]
            mixed.append(dot(pair, partner).astype(BF16))
        result = dot_t(basis[p], jnp.concatenate(mixed, axis=1))
        corner = result[:RANK, :RANK]
        rows = slice(p * RANK, (p + 1) * RANK)
        left[rows, :] = 0.5 * (corner + jnp.transpose(corner))
        right[rows, :] = result[:RANK, RANK : 2 * RANK]
        lifted.append(result[:, RANK:])
    solve_spd(left, right, inverse, parents, RANK)
    for p in range(parents):
        solved = jnp.transpose(right[p * RANK : (p + 1) * RANK, :])
        result = lifted[p][RANK:] - dot3(solved, lifted[p][:RANK])
        for place, d in enumerate((2, 0, 1, 3, 4)):
            out[p, d] = result[:, place * RANK : (place + 1) * RANK]


def upper_level(target, blocks, bases, partners):
    parents = bases.shape[0]
    slots = blocks.shape[1]
    return pl.pallas_call(
        functools.partial(upper_kernel, parents, slots),
        in_specs=[pl.BlockSpec(memory_space=SMEM)] + [pl.BlockSpec(memory_space=VMEM)] * 3,
        out_specs=pl.BlockSpec(memory_space=VMEM),
        out_shape=jax.ShapeDtypeStruct((parents, 5, RANK, RANK), F32),
        scratch_shapes=[
            VMEM((parents, 10, 2 * RANK, RANK), BF16),
            VMEM((parents * RANK, RANK), F32),
            VMEM((parents * RANK, RANK), F32),
            VMEM((parents * PANEL, RANK), F32),
        ],
        compiler_params=PARAMS,
        name="upper_level",
    )(target, blocks, bases, partners)


def per_device(near_blocks, leaf_bases, upper_bases, neighbours):
    leaf_count = near_blocks.shape[0]
    rows = ("node", "trow")
    everyone = ("node", "trow", "tcol")
    leaf_total = leaf_count * lax.axis_size(rows)
    parents_all = leaf_total // 2
    first_leaf = lax.axis_index(rows) * leaf_count
    tcol = lax.axis_index("tcol")
    tcols = lax.axis_size("tcol")
    owned = leaf_count // tcols

    lists = lax.all_to_all(neighbours, "tcol", split_axis=0, concat_axis=1, tiled=True)
    owned_ids = first_leaf + tcol * owned + jnp.arange(owned, dtype=jnp.int32)
    target = 2 * ((lists // 2 - owned_ids[:, None] // 2 + 2) % parents_all) + lists % 2

    own = leaf_bases[:, :, SPARE:]
    before = ring(own[leaf_count - REACH :], rows, 1)
    after = ring(own[:REACH], rows, -1)
    partners = jnp.concatenate([before, own, after], axis=0)
    position = (neighbours - first_leaf + leaf_total // 2) % leaf_total - leaf_total // 2 + REACH

    upper_own = upper_bases[:, :, RANK:]
    upper_partners = jnp.concatenate(
        [ring(upper_own, everyone, 1), upper_own, ring(upper_own, everyone, -1)], axis=0
    )

    high, low = factor(tcol.reshape(1), near_blocks, leaf_bases)
    half = leaf_count // 2
    parts = []
    for part in (high[:half], high[half:]):
        held = part
        for hop in range(tcols - 1):
            got = lax.ppermute(held, "tcol", [(hop, hop + 1)])
            held = jnp.where(tcol == hop + 1, got, held)
        parts.append(held)
    high = jnp.concatenate(parts, axis=0)
    upper, lower = rotate(position, near_blocks, leaf_bases, partners)
    skeleton, packed = reduce_rows(high, low, upper, lower)
    arrived = lax.all_to_all(packed, "tcol", split_axis=0, concat_axis=1, tiled=True)
    upper_skeleton = upper_level(target, arrived, upper_bases, upper_partners)
    return (skeleton, upper_skeleton)


def solution(mesh):
    return jax.shard_map(
        per_device,
        mesh=mesh,
        in_specs=(
            P(("node", "trow"), "tcol", None, None),
            P(("node", "trow"), None, None),
            P(("node", "trow", "tcol"), None, None),
            P(("node", "trow"), "tcol"),
        ),
        out_specs=(
            P(("node", "trow"), "tcol", None, None),
            P(("node", "trow", "tcol"), None, None, None),
        ),
        check_vma=False,
    )
```

```python
import functools

import jax
import jax.numpy as jnp
from jax import lax
from jax.experimental import pallas as pl
from jax.experimental.pallas import tpu as pltpu
from jax.sharding import PartitionSpec as P

BLK = 256
RANK = 128
SPARE = BLK - RANK
REACH = 4
LEAF_PANEL = 64
UPPER_PANEL = 32
LANES = 128
SUB = 8
ITEMS = LANES // SUB
F32 = jnp.float32
BF16 = jnp.bfloat16
VMEM = pltpu.VMEM
SMEM = pltpu.SMEM
PARAMS = pltpu.CompilerParams(vmem_limit_bytes=24 << 20)
TAIL = 16
WHOLE = pl.BlockSpec(memory_space=VMEM)


def ring(array, axes, step, skip=None):
    count = lax.axis_size(axes)
    if skip is None:
        return lax.ppermute(array, axes, [(i, (i + step) % count) for i in range(count)])
    last = lax.axis_size(skip)
    pairs = [
        (i * last + j, (i + step) % count * last + j) for i in range(count) for j in range(1, last)
    ]
    return lax.ppermute(array, axes + (skip,), pairs)


def hbm(x):
    return pltpu.with_memory_space_constraint(x, pltpu.HBM)


def after(x, *others):
    return lax.optimization_barrier((x, *others))[0]


def split(x):
    high = x.astype(BF16)
    return high, (x - high.astype(F32)).astype(BF16)


def dot(a, b):
    return jnp.dot(a, b, preferred_element_type=F32)


def dot_t(a, b):
    return lax.dot_general(a, b, (((0,), (0,)), ((), ())), preferred_element_type=F32)


def dot3(a, b):
    a_high, a_low = split(a)
    b_high, b_low = split(b)
    return dot(
        jnp.concatenate([a_high, a_high, a_low], axis=1),
        jnp.concatenate([b_high, b_low, b_high], axis=0),
    )


def invert_packed(x, order):
    ids = lax.broadcasted_iota(jnp.int32, (order, LANES), 0)
    lane = lax.broadcasted_iota(jnp.int32, (order, LANES), 1)
    item, place = lane % ITEMS, lane // ITEMS
    x = list(x)
    for g in range(order // SUB):
        rows = [jnp.take_along_axis(x[g], item + c * ITEMS, axis=1) for c in range(SUB)]
        for c in range(SUB):
            p = g * SUB + c
            pivot = 1.0 / rows[c][p : p + 1, :]
            here = ids == p
            row = jnp.where(here, 1.0, rows[c])
            for e in range(SUB):
                if e != c:
                    factor_e = rows[e][p : p + 1, :] * pivot
                    rows[e] = jnp.where(here, 0.0, rows[e]) - factor_e * row
            rows[c] = row * pivot
            for h in range(order // SUB):
                if h != g:
                    factor_h = x[h][p : p + 1, :] * pivot
                    x[h] = jnp.where(here, 0.0, x[h]) - factor_h * row
        joined = rows[0]
        for c in range(1, SUB):
            joined = jnp.where(place == c, rows[c], joined)
        x[g] = joined
    return x


def solve_scratch(count, size, panel):
    return [
        VMEM((ITEMS * size, size), F32),
        VMEM((count * size, size), F32),
        VMEM((ITEMS * panel, LANES), F32),
    ]


def solve_spd(left, right, inverse, count, size, order):
    for lo in range(0, size, order):
        hi = lo + order
        last = hi == size
        x = []
        for g in range(order // SUB):
            rows = [left[pl.ds(lo + g * SUB + c, ITEMS, stride=size), :] for c in range(SUB)]
            x.append(jnp.transpose(jnp.concatenate(rows, axis=0))[lo:hi, :])
        x = invert_packed(x, order)
        rest = jnp.zeros((LANES - order, LANES), F32)
        for g in range(order // SUB):
            rows = jnp.transpose(jnp.concatenate([x[g], rest], axis=0))
            for c in range(SUB):
                inverse[pl.ds(g * SUB + c, ITEMS, stride=order), :] = rows[
                    c * ITEMS : (c + 1) * ITEMS, :
                ]
        for item in range(count):
            base = item * size
            rows = slice(base + lo, base + hi)
            panel = right[rows, :]
            if not last:
                panel = jnp.concatenate([left[rows, :], panel], axis=1)
            panel = dot3(inverse[item * order : (item + 1) * order, :order], panel)
            for start, stop in ((0, lo), (hi, size)):
                if start < stop:
                    part = slice(base + start, base + stop)
                    update = dot3(left[part, lo:hi], panel)
                    if not last:
                        left[part, :] -= update[:, :size]
                    right[part, :] -= update[:, -size:]
            if not last:
                left[rows, :] = panel[:, :size]
            right[rows, :] = panel[:, -size:]


def ends_kernel(basis, first, last):
    for end, when in ((first, 0), (last, pl.num_programs(0) - 1)):

        @pl.when(pl.program_id(0) == when)
        def _():
            end[...] = basis[...]


def ends_of(bases):
    count = bases.shape[0]
    shape = (REACH, BLK, RANK)
    return pl.pallas_call(
        ends_kernel,
        grid=(2,),
        in_specs=[pl.BlockSpec(shape, lambda i: (i * (count // REACH - 1), 0, SPARE // RANK))],
        out_specs=[WHOLE] * 2,
        out_shape=[jax.ShapeDtypeStruct(shape, BF16)] * 2,
        compiler_params=PARAMS,
        name="ends",
    )(bases)


def factor_kernel(count, group, owned, tcol, block, basis, *refs):
    outs, (left, right, inverse) = refs[:4], refs[4:]
    step = pl.program_id(0)
    half = owned // 2

    @pl.when(tcol[0] == 0)
    def _():
        for g in range(group):
            turned = dot(block[g], basis[g]).astype(BF16)
            rotated = dot_t(basis[g][:, :SPARE], turned)
            corner = rotated[:, :SPARE]
            where = pl.ds(pl.multiple_of((step * group + g) * SPARE, SPARE), SPARE)
            left[where, :] = 0.5 * (corner + jnp.transpose(corner))
            right[where, :] = rotated[:, SPARE:]

        @pl.when(step == pl.num_programs(0) - 1)
        def _():
            solve_spd(left, right, inverse, count, SPARE, LEAF_PANEL)
            for item in range(count):
                solved = jnp.transpose(right[item * SPARE : (item + 1) * SPARE, :])
                part = item % owned // half
                place = item // owned * half + item % half
                outs[2 * part][place], outs[2 * part + 1][place] = split(solved)

def factor(tcol, near_blocks, bases, owned):
    count = bases.shape[0]
    group = REACH
    half = count // 2
    steps = count // group
    near = lambda i, t: (jnp.where(t[0] == 0, i, 0), 0, 0, 0)
    basis = lambda i, t: (jnp.where(t[0] == 0, i, 0), 0, 0)
    return pl.pallas_call(
        functools.partial(factor_kernel, count, group, owned),
        grid_spec=pltpu.PrefetchScalarGridSpec(
            num_scalar_prefetch=1,
            grid=(steps,),
            in_specs=[
                pl.BlockSpec((group, None, BLK, BLK), near),
                pl.BlockSpec((group, BLK, BLK), basis),
            ],
            out_specs=[WHOLE, pl.BlockSpec((half, RANK, SPARE), lambda i, t: (0, 0, 0))] * 2,
            scratch_shapes=solve_scratch(count, SPARE, LEAF_PANEL),
        ),
        out_shape=[
            jax.ShapeDtypeStruct((half, RANK, SPARE), BF16),
            pltpu.HBM((half, RANK, SPARE), BF16),
        ]
        * 2,
        compiler_params=PARAMS,
        name="factor",
    )(tcol, near_blocks, bases)


def rotate_kernel(slots, owned, position, block, basis, own, before, later, *refs):
    outs, partners = refs[:4], refs[4]
    step = pl.program_id(0)
    count = own.shape[0]
    half = owned // 2

    @pl.when(step == 0)
    def _():
        partners[:REACH] = before[...]
        partners[REACH : REACH + count] = own[...]
        partners[REACH + count :] = later[...]

    for g in range(owned):
        turned = jnp.concatenate(
            [
                dot(block[g, k], partners[position[step * owned + g, k]]).astype(BF16)
                for k in range(slots)
            ],
            axis=1,
        )
        rotated = dot_t(basis[g], turned)
        upper, lower = outs[g // half * 2 : g // half * 2 + 2]
        place = step * half + g % half
        upper[place, :SPARE], upper[place, SPARE:] = split(rotated[:SPARE])
        lower[g % half] = rotated[SPARE:]


def rotate(position, near_blocks, bases, before, later, owned):
    count, slots = near_blocks.shape[:2]
    half = count // 2
    width = slots * RANK
    ends = pl.BlockSpec(before.shape, lambda i: (0, 0, 0))
    return pl.pallas_call(
        functools.partial(rotate_kernel, slots, owned),
        grid=(count // owned,),
        in_specs=[
            pl.BlockSpec(memory_space=SMEM),
            pl.BlockSpec((owned, slots, BLK, BLK), lambda i: (i, 0, 0, 0)),
            pl.BlockSpec((owned, BLK, BLK), lambda i: (i, 0, 0)),
            pl.BlockSpec((count, BLK, RANK), lambda i: (0, 0, SPARE // RANK)),
            ends,
            ends,
        ],
        out_specs=[WHOLE, pl.BlockSpec((owned // 2, RANK, width), lambda i: (i, 0, 0))] * 2,
        out_shape=[
            jax.ShapeDtypeStruct((half, 2 * SPARE, width), BF16),
            pltpu.HBM((half, RANK, width), F32),
        ]
        * 2,
        scratch_shapes=[VMEM((count + 2 * REACH, BLK, RANK), BF16)],
        compiler_params=PARAMS,
        name="rotate",
    )(position, near_blocks, bases, bases, before, later)


def schur(high, low, upper, lower):
    result = lower - dot(jnp.concatenate([high, high], axis=1), upper)
    return result if low is None else result - dot(low, upper[:SPARE])


def reduce_kernel(part, slots, half, places, tcol, target, *refs):
    tcols = len(places)
    highs, (low, upper, lower) = refs[:tcols], refs[tcols : tcols + 3]
    skeleton, rings = refs[-1 - tcols], refs[-tcols:]
    if part == 0:
        bases = refs[tcols + 3]
        parents, order, _ = bases.shape
        for ring_ref in (rings[1], rings[-1]):
            for p in range(parents):
                at = half * slots * RANK + TAIL + p * order
                ring_ref[at : at + order] = bases[p, :, RANK:]

    def fill(high, low):
        row = lax.broadcasted_iota(jnp.int32, (TAIL, RANK), 0)
        for step in range(tcols):
            owner = lax.rem(tcol[0] + step, tcols)
            marks = jnp.zeros((TAIL, RANK), F32)
            for g in range(half):
                leaf = owner * half + g
                result = schur(
                    high[leaf], None if low is None else low[leaf], upper[leaf], lower[leaf]
                )
                for k in range(slots):
                    at = g * slots + k
                    block = result[:, k * RANK : (k + 1) * RANK]
                    skeleton[owner, 0, g, k] = block
                    rings[step][at * RANK : (at + 1) * RANK] = block.astype(BF16)
                    mark = target[(2 * owner + part) * half + g, k].astype(F32)
                    marks = jnp.where(row == at, mark, marks)
            at = half * slots * RANK
            rings[step][at : at + TAIL] = marks.astype(BF16)

    for high, at in zip(highs, places):

        @pl.when(tcol[0] == at)
        def _():
            fill(high, low if at == 0 else None)


def reduce_rows(part, tcol, target, places, highs, low, upper, lower, bases, skeleton):
    half_count, _, width = lower.shape
    slots = width // RANK
    tcols = len(highs)
    half = half_count // tcols
    const = lambda x: pl.BlockSpec(x.shape, lambda i: (0,) * x.ndim)
    operands = [tcol, target, *highs, hbm(low), upper, hbm(lower)]
    in_specs = [pl.BlockSpec(memory_space=SMEM)] * 2 + [WHOLE] * tcols
    in_specs += [const(low), WHOLE, const(lower)]
    rows = half * slots * RANK + TAIL
    lengths = [rows] * tcols
    if part == 0:
        operands.append(bases)
        in_specs.append(const(bases))
        for k in (1, tcols - 1):
            lengths[k] = rows + bases.shape[0] * bases.shape[1]
    aliases = {}
    if skeleton is not None:
        aliases = {len(operands): 0}
        operands.append(skeleton)
        in_specs.append(pl.BlockSpec(memory_space=pl.ANY))
    return pl.pallas_call(
        functools.partial(reduce_kernel, part, slots, half, places),
        grid=(1,),
        in_specs=in_specs,
        out_specs=[
            pl.BlockSpec(
                (tcols, 1, half, slots, RANK, RANK), lambda i: (0, part, 0, 0, 0, 0)
            )
        ]
        + [WHOLE] * tcols,
        out_shape=[jax.ShapeDtypeStruct((tcols, 2, half, slots, RANK, RANK), F32)]
        + [jax.ShapeDtypeStruct((length, RANK), BF16) for length in lengths],
        input_output_aliases=aliases,
        compiler_params=PARAMS,
        name="reduce_rows",
    )(*operands)


def upper_kernel(parent, parents, tcols, slots, tcol, *refs):
    arrivals, (before, later, edge, basis) = refs[:tcols], refs[tcols : tcols + 4]
    out, merged, left, right, inverse = refs[-5:]
    merged[...] = jnp.zeros_like(merged)
    end = 2 * slots * RANK + TAIL
    for arrival in arrivals:
        marks = arrival[end - TAIL : end].astype(F32)
        for a in range(2):
            for j in range(slots):
                at = a * slots + j
                place = marks[at, 0].astype(jnp.int32)
                merged[place, a * RANK : (a + 1) * RANK] = arrival[at * RANK : (at + 1) * RANK]

    def partner(place):
        if 0 <= place < parents:
            return basis[place, :, RANK:]
        beside, outer = (before, 0) if place < 0 else (later, tcols - 1)
        at = place % parents
        rows = slice(end + at * 2 * RANK, end + (at + 1) * 2 * RANK)
        return jnp.where(tcol[0] == outer, edge[at], beside[rows])

    mixed = []
    for d in (2, 0, 1, 3, 4):
        pair = jnp.concatenate([merged[2 * d], merged[2 * d + 1]], axis=1)
        other = basis[parent] if d == 2 else partner(parent + d - 2)
        mixed.append(dot(pair, other).astype(BF16))
    lifted = dot_t(basis[parent], jnp.concatenate(mixed, axis=1))
    corner = lifted[:RANK, :RANK]
    left[:RANK, :] = 0.5 * (corner + jnp.transpose(corner))
    right[...] = lifted[:RANK, RANK : 2 * RANK]
    solve_spd(left, right, inverse, 1, RANK, UPPER_PANEL)
    result = lifted[RANK:, RANK:] - dot3(jnp.transpose(right[...]), lifted[:RANK, RANK:])
    for place, d in enumerate((2, 0, 1, 3, 4)):
        out[0, d] = result[:, place * RANK : (place + 1) * RANK]


def upper_level(parent, slots, tcol, arrivals, beside, bases, result):
    parents = bases.shape[0]
    operands = [tcol, *arrivals, *beside, bases]
    in_specs = [pl.BlockSpec(memory_space=SMEM)] + [WHOLE] * (len(operands) - 1)
    aliases = {}
    if result is not None:
        aliases = {len(operands): 0}
        operands.append(result)
        in_specs.append(pl.BlockSpec(memory_space=pl.ANY))
    return pl.pallas_call(
        functools.partial(upper_kernel, parent, parents, len(arrivals), slots),
        grid=(1,),
        in_specs=in_specs,
        out_specs=pl.BlockSpec((1, 5, RANK, RANK), lambda i: (parent, 0, 0, 0)),
        out_shape=jax.ShapeDtypeStruct((parents, 5, RANK, RANK), F32),
        input_output_aliases=aliases,
        scratch_shapes=[VMEM((10, 2 * RANK, RANK), BF16)] + solve_scratch(1, RANK, UPPER_PANEL),
        compiler_params=PARAMS,
        name="upper_level",
    )(*operands)


def per_device(near_blocks, leaf_bases, upper_bases, neighbours):
    leaf_count = near_blocks.shape[0]
    rows = ("node", "trow")
    everyone = ("node", "trow", "tcol")
    leaf_total = leaf_count * lax.axis_size(rows)
    parents_all = leaf_total // 2
    first_leaf = lax.axis_index(rows) * leaf_count
    place = lax.axis_index("tcol")
    tcol = place.reshape(1)
    tcols = lax.axis_size("tcol")
    owned = leaf_count // tcols

    leaf_ids = first_leaf + jnp.arange(leaf_count, dtype=jnp.int32)
    position = (neighbours - first_leaf + leaf_total // 2) % leaf_total - leaf_total // 2 + REACH
    target = 2 * ((neighbours // 2 - leaf_ids[:, None] // 2 + 2) % parents_all) + neighbours % 2

    near_blocks, leaf_bases = hbm(near_blocks), hbm(leaf_bases)
    first_ends, last_ends = ends_of(leaf_bases)
    before = ring(last_ends, rows, 1, "tcol")
    later = ring(first_ends, rows, -1, "tcol")
    solved = factor(tcol, near_blocks, leaf_bases, owned)

    relay = tcols // 2
    send = lambda array, start, stop: lax.ppermute(array, "tcol", [(start, stop)])
    halves = (solved[0], solved[2])
    middle = [send(array, 0, relay) for array in halves]
    parts = rotate(position, near_blocks, leaf_bases, before, later, owned)
    places = [0, relay, *range(relay + 1, tcols), *range(relay - 1, 0, -1)]
    highs = []
    for local, got in zip(halves, middle):
        got = after(got, *parts)
        held = [local, got]
        for way, stop in ((1, tcols), (-1, 0)):
            array = got
            for at in range(relay + way, stop, way):
                array = send(array, at - way, at)
                held.append(array)
        highs.append(held)

    pairs = []
    for group in range(lax.axis_size(rows)):
        last, first = group * tcols + tcols - 1, (group + 1) * tcols
        first %= lax.axis_size(everyone)
        pairs += [(last, first), (first, last)]
    edge = lax.ppermute(after(upper_bases, *parts)[:, :, RANK:], everyone, pairs)

    skeleton = None
    arrivals = []
    for part in range(2):
        skeleton, *rings = reduce_rows(
            part,
            tcol,
            target,
            tuple(places),
            highs[part],
            solved[2 * part + 1],
            parts[2 * part],
            parts[2 * part + 1],
            upper_bases,
            skeleton,
        )
        arrivals.append(rings[:1])
        for k in range(1, tcols):
            arrivals[part].append(ring(rings[k], ("tcol",), k))

    beside = (arrivals[0][1], arrivals[0][-1], edge)
    result = None
    for part in range(2):
        result = upper_level(
            part, near_blocks.shape[1], tcol, arrivals[part], beside, upper_bases, result
        )
    skeleton = skeleton.reshape((leaf_count,) + skeleton.shape[3:])
    return (skeleton, result)


def solution(mesh):
    return jax.shard_map(
        per_device,
        mesh=mesh,
        in_specs=(
            P(("node", "trow"), "tcol", None, None),
            P(("node", "trow"), None, None),
            P(("node", "trow", "tcol"), None, None),
            P(("node", "trow"), "tcol"),
        ),
        out_specs=(
            P(("node", "trow"), "tcol", None, None),
            P(("node", "trow", "tcol"), None, None, None),
        ),
        check_vma=False,
    )
```

```python
import functools

import jax
import jax.numpy as jnp
from jax import lax
from jax.experimental import pallas as pl
from jax.experimental.pallas import tpu as pltpu
from jax.sharding import PartitionSpec as P

BLK = 256
RANK = 128
SPARE = BLK - RANK
REACH = 4
LEAF_PANEL = 64
UPPER_PANEL = 32
LANES = 128
SUB = 8
ITEMS = LANES // SUB
F32 = jnp.float32
BF16 = jnp.bfloat16
VMEM = pltpu.VMEM
SMEM = pltpu.SMEM
PARAMS = pltpu.CompilerParams(vmem_limit_bytes=24 << 20)
TAIL = 16
WHOLE = pl.BlockSpec(memory_space=VMEM)


def ring(array, axes, step, skip=None):
    count = lax.axis_size(axes)
    if skip is None:
        return lax.ppermute(array, axes, [(i, (i + step) % count) for i in range(count)])
    last = lax.axis_size(skip)
    pairs = [
        (i * last + j, (i + step) % count * last + j) for i in range(count) for j in range(1, last)
    ]
    return lax.ppermute(array, axes + (skip,), pairs)


def hbm(x):
    return pltpu.with_memory_space_constraint(x, pltpu.HBM)


def after(x, *others):
    return lax.optimization_barrier((x, *others))[0]


def split(x):
    high = x.astype(BF16)
    return high, (x - high.astype(F32)).astype(BF16)


def dot(a, b):
    return jnp.dot(a, b, preferred_element_type=F32)


def dot_t(a, b):
    return lax.dot_general(a, b, (((0,), (0,)), ((), ())), preferred_element_type=F32)


def dot3(a, b):
    a_high, a_low = split(a)
    b_high, b_low = split(b)
    return dot(
        jnp.concatenate([a_high, a_high, a_low], axis=1),
        jnp.concatenate([b_high, b_low, b_high], axis=0),
    )


def invert_packed(x, order):
    ids = lax.broadcasted_iota(jnp.int32, (order, LANES), 0)
    lane = lax.broadcasted_iota(jnp.int32, (order, LANES), 1)
    item, place = lane % ITEMS, lane // ITEMS
    x = list(x)
    for g in range(order // SUB):
        rows = [jnp.take_along_axis(x[g], item + c * ITEMS, axis=1) for c in range(SUB)]
        for c in range(SUB):
            p = g * SUB + c
            pivot = 1.0 / rows[c][p : p + 1, :]
            here = ids == p
            row = jnp.where(here, 1.0, rows[c])
            for e in range(SUB):
                if e != c:
                    factor_e = rows[e][p : p + 1, :] * pivot
                    rows[e] = jnp.where(here, 0.0, rows[e]) - factor_e * row
            rows[c] = row * pivot
            for h in range(order // SUB):
                if h != g:
                    factor_h = x[h][p : p + 1, :] * pivot
                    x[h] = jnp.where(here, 0.0, x[h]) - factor_h * row
        joined = rows[0]
        for c in range(1, SUB):
            joined = jnp.where(place == c, rows[c], joined)
        x[g] = joined
    return x


def solve_scratch(count, size, panel):
    return [
        VMEM((ITEMS * size, size), F32),
        VMEM((count * size, size), F32),
        VMEM((ITEMS * panel, LANES), F32),
    ]


def solve_spd(left, right, inverse, count, size, order):
    for lo in range(0, size, order):
        hi = lo + order
        last = hi == size
        x = []
        for g in range(order // SUB):
            rows = [left[pl.ds(lo + g * SUB + c, ITEMS, stride=size), :] for c in range(SUB)]
            x.append(jnp.transpose(jnp.concatenate(rows, axis=0))[lo:hi, :])
        x = invert_packed(x, order)
        rest = jnp.zeros((LANES - order, LANES), F32)
        for g in range(order // SUB):
            rows = jnp.transpose(jnp.concatenate([x[g], rest], axis=0))
            for c in range(SUB):
                inverse[pl.ds(g * SUB + c, ITEMS, stride=order), :] = rows[
                    c * ITEMS : (c + 1) * ITEMS, :
                ]
        for item in range(count):
            base = item * size
            rows = slice(base + lo, base + hi)
            panel = right[rows, :]
            if not last:
                panel = jnp.concatenate([left[rows, :], panel], axis=1)
            panel = dot3(inverse[item * order : (item + 1) * order, :order], panel)
            for start, stop in ((0, lo), (hi, size)):
                if start < stop:
                    part = slice(base + start, base + stop)
                    update = dot3(left[part, lo:hi], panel)
                    if not last:
                        left[part, :] -= update[:, :size]
                    right[part, :] -= update[:, -size:]
            if not last:
                left[rows, :] = panel[:, :size]
            right[rows, :] = panel[:, -size:]


def ends_kernel(basis, first, last):
    for end, when in ((first, 0), (last, pl.num_programs(0) - 1)):

        @pl.when(pl.program_id(0) == when)
        def _():
            end[...] = basis[...]


def ends_of(bases):
    count = bases.shape[0]
    shape = (REACH, BLK, RANK)
    return pl.pallas_call(
        ends_kernel,
        grid=(2,),
        in_specs=[pl.BlockSpec(shape, lambda i: (i * (count // REACH - 1), 0, SPARE // RANK))],
        out_specs=[WHOLE] * 2,
        out_shape=[jax.ShapeDtypeStruct(shape, BF16)] * 2,
        compiler_params=PARAMS,
        name="ends",
    )(bases)


def solve_one(left, right, size, order):
    ids = lax.broadcasted_iota(jnp.int32, (order, 1), 0)
    for lo in range(0, size, order):
        hi = lo + order
        last = hi == size
        x = [left[lo:hi, :], right[lo:hi, :]]
        for s in range(0, order, SUB):
            cols = [
                jnp.broadcast_to(x[0][:, lo + s + c : lo + s + c + 1], (order, LANES))
                for c in range(SUB)
            ]
            for c in range(SUB):
                p = s + c
                pivot = 1.0 / cols[c][p : p + 1, :]
                here = ids == p
                col = jnp.where(here, 0.0, cols[c])
                for e in range(c + 1, SUB):
                    row = cols[e][p : p + 1, :] * pivot
                    cols[e] = jnp.where(here, row, cols[e] - col * row)
                for h in range(2):
                    row = x[h][p : p + 1, :] * pivot
                    x[h] = jnp.where(here, row, x[h] - col * row)
        panel = x[1] if last else jnp.concatenate(x, axis=1)
        for start, stop in ((0, lo), (hi, size)):
            if start < stop:
                update = dot3(left[start:stop, lo:hi], panel)
                if not last:
                    left[start:stop, :] -= update[:, :size]
                right[start:stop, :] -= update[:, -size:]
        if not last:
            left[lo:hi, :] = x[0]
        right[lo:hi, :] = x[1]


def factor_kernel(count, group, owned, tcol, block, basis, *refs):
    outs, (left, right, inverse) = refs[:4], refs[4:]
    step = pl.program_id(0)
    half = owned // 2

    @pl.when(tcol[0] == 0)
    def _():
        for g in range(group):
            turned = dot(block[g], basis[g]).astype(BF16)
            rotated = dot_t(basis[g][:, :SPARE], turned)
            corner = rotated[:, :SPARE]
            where = pl.ds(pl.multiple_of((step * group + g) * SPARE, SPARE), SPARE)
            left[where, :] = 0.5 * (corner + jnp.transpose(corner))
            right[where, :] = rotated[:, SPARE:]

        @pl.when(step == pl.num_programs(0) - 1)
        def _():
            solve_spd(left, right, inverse, count, SPARE, LEAF_PANEL)
            for item in range(count):
                solved = jnp.transpose(right[item * SPARE : (item + 1) * SPARE, :])
                part = item % owned // half
                place = item // owned * half + item % half
                outs[2 * part][place], outs[2 * part + 1][place] = split(solved)

def factor(tcol, near_blocks, bases, owned):
    count = bases.shape[0]
    group = REACH
    half = count // 2
    steps = count // group
    near = lambda i, t: (jnp.where(t[0] == 0, i, 0), 0, 0, 0)
    basis = lambda i, t: (jnp.where(t[0] == 0, i, 0), 0, 0)
    return pl.pallas_call(
        functools.partial(factor_kernel, count, group, owned),
        grid_spec=pltpu.PrefetchScalarGridSpec(
            num_scalar_prefetch=1,
            grid=(steps,),
            in_specs=[
                pl.BlockSpec((group, None, BLK, BLK), near),
                pl.BlockSpec((group, BLK, BLK), basis),
            ],
            out_specs=[WHOLE, pl.BlockSpec((half, RANK, SPARE), lambda i, t: (0, 0, 0))] * 2,
            scratch_shapes=solve_scratch(count, SPARE, LEAF_PANEL),
        ),
        out_shape=[
            jax.ShapeDtypeStruct((half, RANK, SPARE), BF16),
            pltpu.HBM((half, RANK, SPARE), BF16),
        ]
        * 2,
        compiler_params=PARAMS,
        name="factor",
    )(tcol, near_blocks, bases)


def rotate_kernel(slots, owned, position, block, basis, own, before, later, *refs):
    outs, partners = refs[:4], refs[4]
    step = pl.program_id(0)
    count = own.shape[0]
    half = owned // 2

    @pl.when(step == 0)
    def _():
        partners[:REACH] = before[...]
        partners[REACH : REACH + count] = own[...]
        partners[REACH + count :] = later[...]

    for g in range(owned):
        turned = jnp.concatenate(
            [
                dot(block[g, k], partners[position[step * owned + g, k]]).astype(BF16)
                for k in range(slots)
            ],
            axis=1,
        )
        rotated = dot_t(basis[g], turned)
        upper, lower = outs[g // half * 2 : g // half * 2 + 2]
        place = step * half + g % half
        upper[place, :SPARE], upper[place, SPARE:] = split(rotated[:SPARE])
        lower[g % half] = rotated[SPARE:]


def rotate(position, near_blocks, bases, before, later, owned):
    count, slots = near_blocks.shape[:2]
    half = count // 2
    width = slots * RANK
    ends = pl.BlockSpec(before.shape, lambda i: (0, 0, 0))
    return pl.pallas_call(
        functools.partial(rotate_kernel, slots, owned),
        grid=(count // owned,),
        in_specs=[
            pl.BlockSpec(memory_space=SMEM),
            pl.BlockSpec((owned, slots, BLK, BLK), lambda i: (i, 0, 0, 0)),
            pl.BlockSpec((owned, BLK, BLK), lambda i: (i, 0, 0)),
            pl.BlockSpec((count, BLK, RANK), lambda i: (0, 0, SPARE // RANK)),
            ends,
            ends,
        ],
        out_specs=[WHOLE, pl.BlockSpec((owned // 2, RANK, width), lambda i: (i, 0, 0))] * 2,
        out_shape=[
            jax.ShapeDtypeStruct((half, 2 * SPARE, width), BF16),
            pltpu.HBM((half, RANK, width), F32),
        ]
        * 2,
        scratch_shapes=[VMEM((count + 2 * REACH, BLK, RANK), BF16)],
        compiler_params=PARAMS,
        name="rotate",
    )(position, near_blocks, bases, bases, before, later)


def schur(high, low, upper, lower):
    result = lower - dot(jnp.concatenate([high, high], axis=1), upper)
    return result if low is None else result - dot(low, upper[:SPARE])


def reduce_kernel(part, slots, half, places, tcol, target, *refs):
    tcols = len(places)
    highs, (low, upper, lower) = refs[:tcols], refs[tcols : tcols + 3]
    skeleton, rings = refs[-1 - tcols], refs[-tcols:]
    if part == 0:
        bases = refs[tcols + 3]
        parents, order, _ = bases.shape
        for ring_ref in (rings[1], rings[-1]):
            for p in range(parents):
                at = half * slots * RANK + TAIL + p * order
                ring_ref[at : at + order] = bases[p, :, RANK:]

    def fill(high, low):
        row = lax.broadcasted_iota(jnp.int32, (TAIL, RANK), 0)
        for step in range(tcols):
            owner = lax.rem(tcol[0] + step, tcols)
            marks = jnp.zeros((TAIL, RANK), F32)
            for g in range(half):
                leaf = owner * half + g
                result = schur(
                    high[leaf], None if low is None else low[leaf], upper[leaf], lower[leaf]
                )
                for k in range(slots):
                    at = g * slots + k
                    block = result[:, k * RANK : (k + 1) * RANK]
                    skeleton[owner, 0, g, k] = block
                    rings[step][at * RANK : (at + 1) * RANK] = block.astype(BF16)
                    mark = target[(2 * owner + part) * half + g, k].astype(F32)
                    marks = jnp.where(row == at, mark, marks)
            at = half * slots * RANK
            rings[step][at : at + TAIL] = marks.astype(BF16)

    for high, at in zip(highs, places):

        @pl.when(tcol[0] == at)
        def _():
            fill(high, low if at == 0 else None)


def reduce_rows(part, tcol, target, places, highs, low, upper, lower, bases, skeleton):
    half_count, _, width = lower.shape
    slots = width // RANK
    tcols = len(highs)
    half = half_count // tcols
    const = lambda x: pl.BlockSpec(x.shape, lambda i: (0,) * x.ndim)
    operands = [tcol, target, *highs, hbm(low), upper, hbm(lower)]
    in_specs = [pl.BlockSpec(memory_space=SMEM)] * 2 + [WHOLE] * tcols
    in_specs += [const(low), WHOLE, const(lower)]
    rows = half * slots * RANK + TAIL
    lengths = [rows] * tcols
    if part == 0:
        operands.append(bases)
        in_specs.append(const(bases))
        for k in (1, tcols - 1):
            lengths[k] = rows + bases.shape[0] * bases.shape[1]
    aliases = {}
    if skeleton is not None:
        aliases = {len(operands): 0}
        operands.append(skeleton)
        in_specs.append(pl.BlockSpec(memory_space=pl.ANY))
    return pl.pallas_call(
        functools.partial(reduce_kernel, part, slots, half, places),
        grid=(1,),
        in_specs=in_specs,
        out_specs=[
            pl.BlockSpec(
                (tcols, 1, half, slots, RANK, RANK), lambda i: (0, part, 0, 0, 0, 0)
            )
        ]
        + [WHOLE] * tcols,
        out_shape=[jax.ShapeDtypeStruct((tcols, 2, half, slots, RANK, RANK), F32)]
        + [jax.ShapeDtypeStruct((length, RANK), BF16) for length in lengths],
        input_output_aliases=aliases,
        compiler_params=PARAMS,
        name="reduce_rows",
    )(*operands)


def upper_kernel(parent, parents, tcols, slots, tcol, *refs):
    arrivals, (before, later, edge, basis) = refs[:tcols], refs[tcols : tcols + 4]
    out, merged, left, right = refs[-4:]
    merged[...] = jnp.zeros_like(merged)
    end = 2 * slots * RANK + TAIL
    for arrival in arrivals:
        marks = arrival[end - TAIL : end].astype(F32)
        for a in range(2):
            for j in range(slots):
                at = a * slots + j
                place = marks[at, 0].astype(jnp.int32)
                merged[place, a * RANK : (a + 1) * RANK] = arrival[at * RANK : (at + 1) * RANK]

    def partner(place):
        if 0 <= place < parents:
            return basis[place, :, RANK:]
        beside, outer = (before, 0) if place < 0 else (later, tcols - 1)
        at = place % parents
        rows = slice(end + at * 2 * RANK, end + (at + 1) * 2 * RANK)
        return jnp.where(tcol[0] == outer, edge[at], beside[rows])

    mixed = []
    for d in (2, 0, 1, 3, 4):
        pair = jnp.concatenate([merged[2 * d], merged[2 * d + 1]], axis=1)
        other = basis[parent] if d == 2 else partner(parent + d - 2)
        mixed.append(dot(pair, other).astype(BF16))
    lifted = dot_t(basis[parent], jnp.concatenate(mixed, axis=1))
    corner = lifted[:RANK, :RANK]
    left[...] = 0.5 * (corner + jnp.transpose(corner))
    right[...] = lifted[:RANK, RANK : 2 * RANK]
    solve_one(left, right, RANK, UPPER_PANEL)
    result = lifted[RANK:, RANK:] - dot3(jnp.transpose(right[...]), lifted[:RANK, RANK:])
    for place, d in enumerate((2, 0, 1, 3, 4)):
        out[0, d] = result[:, place * RANK : (place + 1) * RANK]


def upper_level(parent, slots, tcol, arrivals, beside, bases, result):
    parents = bases.shape[0]
    operands = [tcol, *arrivals, *beside, bases]
    in_specs = [pl.BlockSpec(memory_space=SMEM)] + [WHOLE] * (len(operands) - 1)
    aliases = {}
    if result is not None:
        aliases = {len(operands): 0}
        operands.append(result)
        in_specs.append(pl.BlockSpec(memory_space=pl.ANY))
    return pl.pallas_call(
        functools.partial(upper_kernel, parent, parents, len(arrivals), slots),
        grid=(1,),
        in_specs=in_specs,
        out_specs=pl.BlockSpec((1, 5, RANK, RANK), lambda i: (parent, 0, 0, 0)),
        out_shape=jax.ShapeDtypeStruct((parents, 5, RANK, RANK), F32),
        input_output_aliases=aliases,
        scratch_shapes=[VMEM((10, 2 * RANK, RANK), BF16)] + [VMEM((RANK, RANK), F32)] * 2,
        compiler_params=PARAMS,
        name="upper_level",
    )(*operands)


def per_device(near_blocks, leaf_bases, upper_bases, neighbours):
    leaf_count = near_blocks.shape[0]
    rows = ("node", "trow")
    everyone = ("node", "trow", "tcol")
    leaf_total = leaf_count * lax.axis_size(rows)
    parents_all = leaf_total // 2
    first_leaf = lax.axis_index(rows) * leaf_count
    place = lax.axis_index("tcol")
    tcol = place.reshape(1)
    tcols = lax.axis_size("tcol")
    owned = leaf_count // tcols

    leaf_ids = first_leaf + jnp.arange(leaf_count, dtype=jnp.int32)
    position = (neighbours - first_leaf + leaf_total // 2) % leaf_total - leaf_total // 2 + REACH
    target = 2 * ((neighbours // 2 - leaf_ids[:, None] // 2 + 2) % parents_all) + neighbours % 2

    near_blocks, leaf_bases = hbm(near_blocks), hbm(leaf_bases)
    first_ends, last_ends = ends_of(leaf_bases)
    before = ring(last_ends, rows, 1, "tcol")
    later = ring(first_ends, rows, -1, "tcol")
    solved = factor(tcol, near_blocks, leaf_bases, owned)

    relay = tcols // 2
    send = lambda array, start, stop: lax.ppermute(array, "tcol", [(start, stop)])
    halves = (solved[0], solved[2])
    middle = [send(array, 0, relay) for array in halves]
    parts = rotate(position, near_blocks, leaf_bases, before, later, owned)
    places = [0, relay, *range(relay + 1, tcols), *range(relay - 1, 0, -1)]
    highs = []
    for local, got in zip(halves, middle):
        got = after(got, *parts)
        held = [local, got]
        for way, stop in ((1, tcols), (-1, 0)):
            array = got
            for at in range(relay + way, stop, way):
                array = send(array, at - way, at)
                held.append(array)
        highs.append(held)

    pairs = []
    for group in range(lax.axis_size(rows)):
        last, first = group * tcols + tcols - 1, (group + 1) * tcols
        first %= lax.axis_size(everyone)
        pairs += [(last, first), (first, last)]
    edge = lax.ppermute(after(upper_bases, *parts)[:, :, RANK:], everyone, pairs)
    target = after(target, edge)

    skeleton = None
    arrivals = []
    for part in range(2):
        skeleton, *rings = reduce_rows(
            part,
            tcol,
            target,
            tuple(places),
            highs[part],
            solved[2 * part + 1],
            parts[2 * part],
            parts[2 * part + 1],
            upper_bases,
            skeleton,
        )
        arrivals.append(rings[:1])
        for k in range(1, tcols):
            arrivals[part].append(ring(rings[k], ("tcol",), k))

    beside = (arrivals[0][1], arrivals[0][-1], edge)
    result = None
    for part in range(2):
        result = upper_level(
            part, near_blocks.shape[1], tcol, arrivals[part], beside, upper_bases, result
        )
    skeleton = skeleton.reshape((leaf_count,) + skeleton.shape[3:])
    return (skeleton, result)


def solution(mesh):
    return jax.shard_map(
        per_device,
        mesh=mesh,
        in_specs=(
            P(("node", "trow"), "tcol", None, None),
            P(("node", "trow"), None, None),
            P(("node", "trow", "tcol"), None, None),
            P(("node", "trow"), "tcol"),
        ),
        out_specs=(
            P(("node", "trow"), "tcol", None, None),
            P(("node", "trow", "tcol"), None, None, None),
        ),
        check_vma=False,
    )
```
